32 devices in a mesh: groups: 2 (over y), lat: 16 (over z, x, core).
Axes of the slice: x: 2, y: 2, z: 4, core: 2. Of those that a mesh axis runs over, the one named last changes fastest.
Arguments:
- acts: bfloat16 [32768, 128], P(('groups', 'lat')), parts along dimension 0, may hold values from -6 to 6
- mask: int32 [3072, 128], P(('groups', 'lat')), parts along dimension 0, may hold values from 0 to 3
- enc_weight: bfloat16 [3072, 16384], P(('groups', 'lat')), parts along dimension 0, may hold values from -0.046875 to 0.046875
- enc_bias: float32 [3072], P(('groups', 'lat')), parts along dimension 0, may hold values from -3 to 3
- threshold: float32 [3072], P(('groups', 'lat')), parts along dimension 0, may hold values from 0.05 to 0.5
- dec_weight: bfloat16 [3072, 16384], P(('groups', 'lat')), parts along dimension 0, may hold values from -0.21875 to 0.21875
- dec_bias: float32 [32768], P(('groups', 'lat')), parts along dimension 0, may hold values from -3 to 3
Outputs:
- grad_enc: bfloat16 [3072, 16384], P(('groups', 'lat')), parts along dimension 0
- grad_enc_bias: float32 [3072], P(('groups', 'lat')), parts along dimension 0
- grad_theta: float32 [3072], P(('groups', 'lat')), parts along dimension 0
- grad_dec: bfloat16 [3072, 16384], P(('groups', 'lat')), parts along dimension 0
- grad_dec_bias: float32 [32768], P(('groups', 'lat')), parts along dimension 0
The draws below stay inside these ranges and needn't reach their ends.
There are 2 independent parts, one for each index of `groups`. The reference program is written for one: setup_inputs(seed, part) draws one part's arguments, and reference() takes and returns one part's arrays. A program takes and returns all parts, laid end to end along the dimension named above; each array names one. Nothing has to cross between parts.
Inputs may be any that keep to these rules, and one draw needn't show every extreme that they name: mask % 2 is 1 where a latent's JumpReLU gate is open for a token; mask // 2 is 1 where the token lies inside that latent's threshold window.
All inputs are finite; a program needn't handle non-finite values.
Results may differ from the reference program's by a relative error of at most 0.0058.
Values may be sent and summed in bfloat16 or wider, within the bound.
A program may use at most 64 MiB of HBM per device.

```python
import math
import jax
import jax.numpy as jnp
from jax import lax

D = 8192
TOK = 128
L = 1536


def set_ends(values, stream_key, low, largest):
    spot = [jax.random.randint(jax.random.fold_in(stream_key, axis), (), 0, length) for axis, length in enumerate(values.shape)]
    main_axis = values.shape.index(max(values.shape))
    next_to = spot[:main_axis] + [(spot[main_axis] + 1) % values.shape[main_axis]] + spot[main_axis + 1:]
    return values.at[tuple(spot)].set(low).at[tuple(next_to)].set(largest)


def with_spikes(result, key, source, target, parts, factor):
    owner, partner = [(jnp.arange(result.shape[dim]) // (result.shape[dim] // parts)).reshape([-1 if axis == dim else 1 for axis in range(result.ndim)]) for dim in (source, target)]
    chosen = jax.random.permutation(key, parts)[partner]
    strong = (owner == chosen) | (owner == (partner + parts // 2) % parts)
    return jnp.where(strong, factor * result, result)


def block_scale(key, shape, pieces, least, high):
    loudness, own = 1.0, jax.random.fold_in(key, 6)
    for axis_at, shards_of in pieces:
        draws = jnp.exp(jax.random.uniform(jax.random.fold_in(own, axis_at), (shards_of,), jnp.float32, least / len(pieces), high / len(pieces)))
        loudness = loudness * jnp.repeat(draws, shape[axis_at] // shards_of).reshape([-1 if axis == axis_at else 1 for axis in range(len(shape))])
    return loudness


def bell_draw(own_key, extent, scale, most, cuts=(), held_as=jnp.bfloat16):
    factor_of = block_scale(own_key, extent, cuts, -0.22, 0.18) if cuts else 1.0
    array = jax.random.normal(own_key, extent, jnp.float32) * scale * factor_of
    return jnp.minimum(jnp.maximum(array, -most), most).astype(held_as)


def heavy_noise(rng, shape, width, limit, cuts, heavy, held_as=jnp.bfloat16):
    values = width * jax.random.normal(rng, shape, jnp.float32)
    if cuts:
        values = values * block_scale(rng, shape, cuts, -0.22, 0.18)
    return jnp.clip(with_spikes(values, jax.random.fold_in(rng, 3), *heavy), -limit, limit).astype(held_as)


def setup_inputs(seed: int = 0, part: int = 0) -> dict:
    arg_keys = jax.random.split(jax.random.key(seed), 8)
    part_splits = jax.random.split(jax.random.fold_in(arg_keys[7], part), 8)
    acts = bell_draw(part_splits[0], (2 * D, TOK), 1.0, 6.0, ((0, 16),))
    mask = set_ends(jax.random.randint(part_splits[1], (L, TOK), 0, 4), jax.random.fold_in(part_splits[1], 1), 0, 3).astype(jnp.int32)
    enc_weight = bell_draw(part_splits[2], (L, 2 * D), (2 * D) ** -0.5, 0.046875, ((0, 16),))
    enc_bias = bell_draw(part_splits[3], (L,), 0.5, 3.0, ((0, 16),), jnp.float32)
    threshold = jnp.clip(jnp.exp(math.log(0.5) - 2.3025851 * jax.random.uniform(part_splits[4], (L,), jnp.float32) ** block_scale(part_splits[4], (L,), ((0, 16),), -0.2, 0.2)), 0.05, 0.5)
    dec_weight = heavy_noise(part_splits[5], (L, 2 * D), L ** -0.5, 0.21875, ((0, 16),), (0, 1, 16, 2.0))
    dec_bias = bell_draw(part_splits[6], (2 * D,), 0.5, 3.0, ((0, 16),), jnp.float32)
    return dict(acts=acts, mask=mask, enc_weight=enc_weight, enc_bias=enc_bias, threshold=threshold, dec_weight=dec_weight, dec_bias=dec_bias)


sparsity_coef = 0.1
spread = 0.1
norm_eps = 1e-06

def reference(acts, mask, enc_weight, enc_bias, threshold, dec_weight, dec_bias):
    scale = 1.0 / math.sqrt(TOK)
    pre = jnp.dot(enc_weight, acts, preferred_element_type=jnp.float32) + enc_bias[:, None]
    active = (mask % 2).astype(jnp.float32)
    window = (mask // 2).astype(jnp.float32)
    feats = (active * pre).astype(jnp.bfloat16)
    recon = jnp.dot(dec_weight.T, feats, preferred_element_type=jnp.float32)
    error = (recon + dec_bias[:, None] - acts.astype(jnp.float32)).astype(jnp.bfloat16)
    wide = dec_weight.astype(jnp.float32)
    norm_base = jnp.sqrt(lax.optimization_barrier(jnp.sum(wide[:, :D] * wide[:, :D], axis=1)) + norm_eps)
    norm_adjusted = jnp.sqrt(lax.optimization_barrier(jnp.sum(wide[:, D:] * wide[:, D:], axis=1)) + norm_eps)
    weight_sum = norm_base + norm_adjusted
    grec = jnp.dot(dec_weight, error, preferred_element_type=jnp.float32)
    gpre = (active * grec).astype(jnp.bfloat16)
    dims = (((1,), (1,)), ((), ()))
    grad_enc = (scale * lax.dot_general(gpre, acts, dims, preferred_element_type=jnp.float32)).astype(jnp.bfloat16)
    grad_enc_bias = scale * lax.optimization_barrier(jnp.sum(gpre.astype(jnp.float32), axis=1))
    grad_theta = -(scale / spread) * lax.optimization_barrier(jnp.sum(window * (threshold[:, None] * grec + sparsity_coef * weight_sum[:, None]), axis=1))
    counts = lax.optimization_barrier(jnp.sum(active, axis=1))
    cross = lax.dot_general(feats, error, dims, preferred_element_type=jnp.float32)
    unit = jnp.concatenate([wide[:, :D] / norm_base[:, None], wide[:, D:] / norm_adjusted[:, None]], axis=1)
    grad_dec = (scale * (cross + sparsity_coef * counts[:, None] * unit)).astype(jnp.bfloat16)
    grad_dec_bias = scale * lax.optimization_barrier(jnp.sum(error.astype(jnp.float32), axis=1))
    return (grad_enc, grad_enc_bias, grad_theta, grad_dec, grad_dec_bias)
```

```python
import functools
import math

import jax
import jax.numpy as jnp
from jax import lax
from jax.experimental import pallas as pl
from jax.experimental.pallas import tpu as pltpu
from jax.sharding import PartitionSpec as P

sparsity_coef = 0.1
spread = 0.1
norm_eps = 1e-06

MESH = pl.DeviceIdType.MESH
f32 = jnp.float32
bf16 = jnp.bfloat16


def lat_shape(lat):
    chips = lat // 2
    nx = 1
    while (2 * nx) ** 3 <= chips:
        nx *= 2
    return chips // nx, nx


def dot(a, b, dims):
    return lax.dot_general(a, b, (dims, ((), ())), preferred_element_type=f32)


NN = ((1,), (0,))
NT = ((1,), (1,))
TN = ((0,), (0,))


def kernel(
    nz, nx, scale,
    acts_ref, mask_ref, encb_ref, thr_ref, decb_ref, enc_hbm, dec_hbm,
    ge_out, geb_out, gth_out, gd_out, gdb_out,
    enc_v, dec_v, cat, abuf, ebuf, feats2, pre_v, grec_v, gpre_v, coef_v,
    bsend, brecv, csend, crecv, gd_v, ge_v, actst,
    load_sems, dsend, drecv, fsem,
    a_up, a_x, a_sib, a_recv, e_up, e_x, e_sib, e_recv,
    b_s, b_r, c_s, c_r, gd_sem, ge_sem,
):
    n = 2 * nz * nx
    rows = mask_ref.shape[0]
    fb = acts_ref.shape[0]
    me = lax.axis_index("lat")
    c = lax.rem(me, 2)
    x = lax.rem(me // 2, nx)
    z = me // (2 * nx)
    sib = me + 1 - 2 * c

    def at(zz, xx, cc):
        return (zz * nx + xx) * 2 + cc

    def shifted_x(d):
        return lax.rem(x + d, nx)

    def cols(i, width=fb):
        return pl.ds(pl.multiple_of(i * fb, 128), width)

    short = jnp.minimum(z, nz - 1 - z)
    upper = (2 * z < nz - 1).astype(jnp.int32)

    def kth(k):
        if k == 0:
            return z
        paired = z - (k + 1) // 2 if k % 2 else z + k // 2
        alone = z + (2 * upper - 1) * (k - short)
        both = (k <= 2 * short).astype(jnp.int32)
        return both * paired + (1 - both) * alone

    barrier = pltpu.get_barrier_semaphore()

    def greet(device):
        pl.semaphore_signal(barrier, inc=1, device_id={"lat": device}, device_id_type=MESH)

    has_down = z >= 1
    has_up = z <= nz - 2

    @pl.when(has_down)
    def _():
        greet(at(z - 1, x, c))

    @pl.when(has_up)
    def _():
        greet(at(z + 1, x, c))

    for d in range(1, nx):
        greet(at(z, shifted_x(d), c))
    greet(sib)

    loads = [
        pltpu.make_async_copy(enc_hbm, enc_v, load_sems.at[0]),
        pltpu.make_async_copy(dec_hbm, dec_v, load_sems.at[1]),
    ]
    for load in loads:
        load.start()

    pl.semaphore_wait(barrier, nx + has_down.astype(jnp.int32) + has_up.astype(jnp.int32))

    def remote(src, dst, send, recv, device):
        return pltpu.make_async_remote_copy(
            src_ref=src, dst_ref=dst, send_sem=send, recv_sem=recv,
            device_id={"lat": device}, device_id_type=MESH,
        )

    def block_copy(buf, i, send, recv, device):
        return remote(buf.at[i], buf.at[i], send, recv.at[i], device)

    def gather(buf, up_s, x_s, sib_s, recv, consume, first=None):
        def z_sends(k, zz):
            i = at(zz, x, c)
            go_up = jnp.logical_and(zz <= z, has_up)
            go_down = jnp.logical_and(zz >= z, has_down)
            return (
                (go_up, block_copy(buf, i, up_s.at[2 * k], recv, at(z + 1, x, c))),
                (go_down, block_copy(buf, i, up_s.at[2 * k + 1], recv, at(z - 1, x, c))),
            )

        def x_send(k, zz, d):
            return block_copy(buf, at(zz, x, c), x_s.at[k * nx + d], recv, at(z, shifted_x(d), c))

        def sib_send(k, zz, d):
            return block_copy(buf, at(zz, shifted_x(d), c), sib_s.at[k * nx + d], recv, sib)

        def arrived(i):
            block_copy(buf, i, sib_s.at[0], recv, sib).wait_recv()

        def step_z(k):
            zz = kth(k)
            if k:
                arrived(at(zz, x, c))
            for go, copy in z_sends(k, zz):
                @pl.when(go)
                def _(copy=copy):
                    copy.start()
            for d in range(1, nx):
                x_send(k, zz, d).start()
            sib_send(k, zz, 0).start()

        def step_x(k):
            zz = kth(k)
            for d in range(1, nx):
                arrived(at(zz, shifted_x(d), c))
                sib_send(k, zz, d).start()

        def step_sib(k):
            zz = kth(k)
            for d in range(nx):
                arrived(at(zz, shifted_x(d), 1 - c))
            consume(k, zz)

        for k in range(nz + 2):
            if k < nz:
                step_z(k)
            if k == 0 and first is not None:
                first()
            if 0 <= k - 1 < nz:
                step_x(k - 1)
            if 0 <= k - 2 < nz:
                step_sib(k - 2)

        for k in range(nz):
            zz = kth(k)
            for go, copy in z_sends(k, zz):
                @pl.when(go)
                def _(copy=copy):
                    copy.wait_send()
            for d in range(1, nx):
                x_send(k, zz, d).wait_send()
            for d in range(nx):
                sib_send(k, zz, d).wait_send()

    abuf[me] = acts_ref[...]

    def dec_send(q):
        return remote(
            dec_hbm.at[:, cols(2 * q + 1 - c)], cat.at[q, pl.ds(rows, rows), :],
            dsend.at[q], drecv.at[q], sib,
        )

    def dec_own(q):
        return pltpu.make_async_copy(
            dec_hbm.at[:, cols(2 * q + c)], cat.at[q, pl.ds(0, rows), :], load_sems.at[2 + q]
        )

    def eye():
        i = lax.broadcasted_iota(jnp.int32, (rows, rows), 0)
        j = lax.broadcasted_iota(jnp.int32, (rows, rows), 1)
        return i == j

    def column(row):
        return jnp.sum(jnp.where(eye(), jnp.broadcast_to(row, (rows, rows)), 0.0), axis=1, keepdims=True)

    def row_of(col):
        return jnp.sum(jnp.where(eye(), jnp.broadcast_to(col, (rows, rows)), 0.0), axis=0, keepdims=True)

    slab = 2 * nx

    def start_rest():
        for q in range(nz * nx):
            dec_own(q).start()
            dec_send(q).start()
        actst[...] = acts_ref[...].astype(f32).T
        pre_v[...] = jnp.zeros_like(pre_v)
        for load in loads:
            load.wait()

    def consume_acts(k, zz):
        def body(j, acc):
            i = zz * slab + j
            return acc + dot(enc_v[:, cols(i)], abuf[i], NN)
        pre_v[...] = lax.fori_loop(0, slab, body, pre_v[...], unroll=True)
        if k == 0:
            half = n // 2
            norms = []
            for m in range(2):
                def square(j, acc):
                    w = dec_v[:, cols(m * half + j)].astype(f32)
                    w = w * w
                    for t in range(fb // 128):
                        acc = acc + w[:, t * 128:(t + 1) * 128]
                    return acc
                acc = lax.fori_loop(0, half, square, jnp.zeros((rows, 128), f32))
                norms.append(jnp.sqrt(jnp.sum(acc, axis=1, keepdims=True) + norm_eps))
            active = lax.rem(mask_ref[...], 2).astype(f32)
            count = jnp.sum(active, axis=1, keepdims=True)
            lane = lax.broadcasted_iota(jnp.int32, (rows, 128), 1)
            coef_v[...] = jnp.where(
                lane == 0, sparsity_coef * count / norms[0],
                jnp.where(lane == 1, sparsity_coef * count / norms[1], norms[0] + norms[1]),
            )

    gather(abuf, a_up, a_x, a_sib, a_recv, consume_acts, start_rest)

    active = lax.rem(mask_ref[...], 2).astype(f32)
    pre = pre_v[...] + column(encb_ref[...])
    feats = (active * pre).astype(bf16)
    feats2[pl.ds(0, rows), :] = feats
    fcopy = remote(
        feats2.at[pl.ds(0, rows), :], feats2.at[pl.ds(rows, rows), :], fsem.at[0], fsem.at[1], sib
    )
    fcopy.start()
    for q in range(nz * nx):
        dec_own(q).wait()
        dec_send(q).wait()
    fcopy.wait()

    both = feats2[...]

    def partial(q):
        return dot(both, cat[q], TN)

    def b_copy(k, zz, d):
        return remote(
            bsend.at[k * nx + d], brecv.at[zz * nx + d], b_s.at[k * nx + d], b_r.at[zz * nx + d],
            at(z, shifted_x(d), c),
        )

    order = list(range(nz - 1, -1, -1))
    for k in order:
        zz = kth(k)
        for d in range(1, nx):
            bsend[k * nx + d] = partial(zz * nx + shifted_x(d)).astype(bf16)
            b_copy(k, zz, d).start()

    def c_copies(k, zz):
        down_slot = zz + (nz - zz) * (zz == z - 1).astype(jnp.int32)
        return (
            (zz > z, remote(csend.at[k], crecv.at[zz], c_s.at[k], c_r.at[zz], at(z + 1, x, c))),
            (zz < z, remote(csend.at[k], crecv.at[down_slot], c_s.at[k], c_r.at[down_slot], at(z - 1, x, c))),
        )

    def c_wait(slot):
        remote(csend.at[0], crecv.at[slot], c_s.at[0], c_r.at[slot], sib).wait_recv()

    total = actst
    for k in order:
        zz = kth(k)
        part = partial(zz * nx + x)
        for d in range(1, nx):
            b_copy(k, zz, d).wait_recv()
            part = part + brecv[zz * nx + d].astype(f32)
        if k:
            csend[k] = part.astype(bf16)
            farther = jnp.logical_or(
                jnp.logical_and(zz > z, has_down), jnp.logical_and(zz < z, has_up)
            )

            @pl.when(farther)
            def _(part=part, zz=zz, k=k):
                c_wait(zz)
                csend[k] = (part + crecv[zz].astype(f32)).astype(bf16)

            for go, copy in c_copies(k, zz):
                @pl.when(go)
                def _(copy=copy):
                    copy.start()
        else:
            total[...] = part + decb_ref[...] - total[...]

            @pl.when(has_down)
            def _():
                c_wait(z)
                total[...] += crecv[z].astype(f32)

            @pl.when(has_up)
            def _():
                c_wait(nz)
                total[...] += crecv[nz].astype(f32)

    error = total[...].astype(bf16)
    ebuf[me] = error

    def gd_copy(zz):
        w = cols(zz * slab, slab * fb)
        return pltpu.make_async_copy(gd_v.at[:, w], gd_out.at[:, w], gd_sem.at[zz])

    def finish_sums():
        gdb_out[...] = scale * jnp.sum(ebuf[me].astype(f32), axis=0, keepdims=True)
        grec_v[...] = jnp.zeros_like(grec_v)
        for k in range(nz):
            zz = kth(k)
            for d in range(1, nx):
                b_copy(k, zz, d).wait_send()
            if k:
                for go, copy in c_copies(k, zz):
                    @pl.when(go)
                    def _(copy=copy):
                        copy.wait_send()

    def consume_errors(k, zz):
        own = feats2[pl.ds(0, rows), :]

        def body(j, acc):
            i = zz * slab + j
            e = ebuf[i]
            w = dec_v[:, cols(i)]
            acc = acc + dot(w, e, NT)
            adjusted = (i >= n // 2).astype(f32)
            coef = coef_v[:, 0:1] + adjusted * (coef_v[:, 1:2] - coef_v[:, 0:1])
            gd_v[:, cols(i)] = (scale * (dot(own, e, NN) + coef * w.astype(f32))).astype(bf16)
            return acc

        grec_v[...] = lax.fori_loop(0, slab, body, grec_v[...])
        gd_copy(zz).start()

    gather(ebuf, e_up, e_x, e_sib, e_recv, consume_errors, finish_sums)

    grec = grec_v[...]
    active = lax.rem(mask_ref[...], 2).astype(f32)
    gpre = (active * grec).astype(bf16)
    gpre_v[...] = gpre

    def ge_copy(zz):
        w = cols(zz * slab, slab * fb)
        return pltpu.make_async_copy(ge_v.at[:, w], ge_out.at[:, w], ge_sem.at[zz])

    for zz in range(nz):
        def body(j, _):
            i = zz * slab + j
            ge_v[:, cols(i)] = (scale * dot(gpre_v[...], abuf[i], NT)).astype(bf16)
            return 0
        lax.fori_loop(0, slab, body, 0)
        ge_copy(zz).start()

    window = (mask_ref[...] // 2).astype(f32)
    theta = window * (column(thr_ref[...]) * grec + sparsity_coef * coef_v[:, 2:3])
    gth_out[...] = row_of(-(scale / spread) * jnp.sum(theta, axis=1, keepdims=True))
    geb_out[...] = row_of(scale * jnp.sum(gpre.astype(f32), axis=1, keepdims=True))
    for zz in range(nz):
        ge_copy(zz).wait()
        gd_copy(zz).wait()


def per_device(lat, acts, mask, enc_weight, enc_bias, threshold, dec_weight, dec_bias):
    nz, nx = lat_shape(lat)
    n = lat
    rows, tokens = mask.shape
    fb = acts.shape[0]
    width = dec_weight.shape[1]
    scale = 1.0 / math.sqrt(tokens)
    vmem = pl.BlockSpec(memory_space=pltpu.VMEM)
    hbm = pl.BlockSpec(memory_space=pl.ANY)
    dma = pltpu.SemaphoreType.DMA
    outs = pl.pallas_call(
        functools.partial(kernel, nz, nx, scale),
        out_shape=(
            jax.ShapeDtypeStruct((rows, width), bf16),
            jax.ShapeDtypeStruct((1, rows), f32),
            jax.ShapeDtypeStruct((1, rows), f32),
            jax.ShapeDtypeStruct((rows, width), bf16),
            jax.ShapeDtypeStruct((1, fb), f32),
        ),
        in_specs=[vmem] * 5 + [hbm] * 2,
        out_specs=(hbm, vmem, vmem, hbm, vmem),
        scratch_shapes=[
            pltpu.VMEM((rows, width), bf16),
            pltpu.VMEM((rows, width), bf16),
            pltpu.VMEM((nz * nx, 2 * rows, fb), bf16),
            pltpu.VMEM((n, fb, tokens), bf16),
            pltpu.VMEM((n, tokens, fb), bf16),
            pltpu.VMEM((2 * rows, tokens), bf16),
            pltpu.VMEM((rows, tokens), f32),
            pltpu.VMEM((rows, tokens), f32),
            pltpu.VMEM((rows, tokens), bf16),
            pltpu.VMEM((rows, 128), f32),
            pltpu.VMEM((nz * nx, tokens, fb), bf16),
            pltpu.VMEM((nz * nx, tokens, fb), bf16),
            pltpu.VMEM((nz, tokens, fb), bf16),
            pltpu.VMEM((nz + 1, tokens, fb), bf16),
            pltpu.VMEM((rows, width), bf16),
            pltpu.VMEM((rows, width), bf16),
            pltpu.VMEM((tokens, fb), f32),
            dma((2 + nz * nx,)), dma((nz * nx,)), dma((nz * nx,)), dma((2,)),
            dma((2 * nz,)), dma((nz * nx,)), dma((nz * nx,)), dma((n,)),
            dma((2 * nz,)), dma((nz * nx,)), dma((nz * nx,)), dma((n,)),
            dma((nz * nx,)), dma((nz * nx,)), dma((nz,)), dma((nz + 1,)),
            dma((nz,)), dma((nz,)),
        ],
        compiler_params=pltpu.CompilerParams(
            collective_id=0, has_side_effects=True, vmem_limit_bytes=56 * 1024 * 1024
        ),
        name="crosscoder",
    )(
        acts, mask, enc_bias.reshape(1, rows), threshold.reshape(1, rows),
        dec_bias.reshape(1, fb), enc_weight, dec_weight,
    )
    ge, geb, gth, gd, gdb = outs
    return ge, geb.reshape(rows), gth.reshape(rows), gd, gdb.reshape(fb)


def solution(mesh):
    wide, flat = P(("groups", "lat"), None), P(("groups", "lat"))
    return jax.shard_map(
        functools.partial(per_device, mesh.shape["lat"]), mesh=mesh,
        in_specs=(wide, wide, wide, flat, flat, wide, flat),
        out_specs=(wide, flat, flat, wide, flat), check_vma=False,
    )
```

```python
import functools
import math

import jax
import jax.numpy as jnp
from jax import lax
from jax.experimental import pallas as pl
from jax.experimental.pallas import tpu as pltpu
from jax.sharding import PartitionSpec as P

sparsity_coef = 0.1
spread = 0.1
norm_eps = 1e-06

MESH = pl.DeviceIdType.MESH
f32 = jnp.float32
bf16 = jnp.bfloat16


def lat_shape(lat):
    chips = lat // 2
    nx = 1
    while (2 * nx) ** 3 <= chips:
        nx *= 2
    return chips // nx, nx


def dot(a, b, dims):
    return lax.dot_general(a, b, (dims, ((), ())), preferred_element_type=f32)


NN = ((1,), (0,))
NT = ((1,), (1,))
TN = ((0,), (0,))


def kernel(
    nz, nx, parts, scale,
    acts_hbm, mask_hbm, encb_hbm, thr_hbm, decb_hbm, enc_hbm, dec_hbm,
    acts_out, gpre_out, geb_out, gth_out, gd_out, gdb_out,
    acts_ref, mask_ref, encb_ref, thr_ref, decb_ref, enc_v, dec_v, cat, abuf, ebuf, feats2, pre_v, grec_v, coef_v,
    bsend, brecv, csend, crecv, cpart, gd_v, actst,
    load_sems, dsend, drecv, fsem,
    a_up, a_x, a_sib, a_recv, e_up, e_x, e_sib, e_recv,
    b_s, b_r, c_s, c_r, gd_sem, out_sem,
):
    n = 2 * nz * nx
    rows = mask_hbm.shape[0]
    fb, tokens = acts_hbm.shape
    lag = 2 * parts
    me = lax.axis_index("lat")
    c = lax.rem(me, 2)
    x = lax.rem(me // 2, nx)
    z = me // (2 * nx)
    sib = me + 1 - 2 * c

    def at(zz, xx, cc):
        return (zz * nx + xx) * 2 + cc

    def shifted_x(d):
        return lax.rem(x + d, nx)

    def cols(i, width=fb):
        return pl.ds(pl.multiple_of(i * fb, 128), width)

    short = jnp.minimum(z, nz - 1 - z)
    upper = (2 * z < nz - 1).astype(jnp.int32)
    blocks, events = nz * parts, (nz - 1) * parts

    def place(paired, p, w, k, g):
        paired = paired.astype(jnp.int32)
        zz = paired * (z + (p + 1) * (2 * (w % 2) - 1)) + (1 - paired) * (z + (2 * upper - 1) * (k - short))
        k = paired * (2 * p + 1 + w % 2) + (1 - paired) * k
        g = paired * (w // 2) + (1 - paired) * g
        return k, zz, g

    def nearest_first(e):
        p, w = e // (2 * parts), e % (2 * parts)
        return place(p < short, p, w, 1 + e // parts, e % parts)

    def farthest_first(e):
        alone = (nz - 1 - 2 * short) * parts
        rest = jnp.maximum(e - alone, 0)
        p, w = short - 1 - rest // (2 * parts), rest % (2 * parts)
        return place(e >= alone, p, w, nz - 1 - e // parts, e % parts)

    def kth(k):
        if k == 0:
            return z
        paired = z - (k + 1) // 2 if k % 2 else z + k // 2
        alone = z + (2 * upper - 1) * (k - short)
        both = (k <= 2 * short).astype(jnp.int32)
        return both * paired + (1 - both) * alone

    def loop(count, body):
        def step(i, carry):
            body(i)
            return carry
        lax.fori_loop(0, count, step, 0)

    barrier = pltpu.get_barrier_semaphore()

    def greet(device):
        pl.semaphore_signal(barrier, inc=1, device_id={"lat": device}, device_id_type=MESH)

    has_down = z >= 1
    has_up = z <= nz - 2

    @pl.when(has_down)
    def _():
        greet(at(z - 1, x, c))

    @pl.when(has_up)
    def _():
        greet(at(z + 1, x, c))

    for d in range(1, nx):
        greet(at(z, shifted_x(d), c))
    greet(sib)

    acts_load, *loads = [
        pltpu.make_async_copy(src, dst, load_sems.at[nz * nx + i])
        for i, (src, dst) in enumerate((
            (acts_hbm, acts_ref), (mask_hbm, mask_ref), (encb_hbm, encb_ref), (thr_hbm, thr_ref),
            (decb_hbm, decb_ref), (enc_hbm, enc_v), (dec_hbm, dec_v),
        ))
    ]
    acts_load.start()
    for load in loads:
        load.start()
    acts_load.wait()
    actst[...] = acts_ref[...].astype(f32).T
    abuf[me] = actst[...].astype(bf16)

    pl.semaphore_wait(barrier, nx + has_down.astype(jnp.int32) + has_up.astype(jnp.int32))

    def remote(src, dst, send, recv, device):
        return pltpu.make_async_remote_copy(
            src_ref=src, dst_ref=dst, send_sem=send, recv_sem=recv,
            device_id={"lat": device}, device_id_type=MESH,
        )

    def gather(buf, up_s, x_s, sib_s, recv, consume, prepare, first=None):
        piece = buf.shape[1] // parts

        def copy_of(i, g, send, device):
            view = buf.at[i, pl.ds(pl.multiple_of(g * piece, piece), piece), :]
            return remote(view, view, send, recv.at[i, g], device)

        def event(e):
            k, zz, g = nearest_first(jnp.maximum(e - parts, 0))
            own = (e < parts).astype(jnp.int32)
            return zz + own * (z - zz), g + own * (e - g)

        def z_sends(e, zz, g):
            i = at(zz, x, c)
            go_up = jnp.logical_and(zz <= z, has_up)
            go_down = jnp.logical_and(zz >= z, has_down)
            return (
                (go_up, copy_of(i, g, up_s.at[0, e], at(z + 1, x, c))),
                (go_down, copy_of(i, g, up_s.at[1, e], at(z - 1, x, c))),
            )

        def x_send(e, zz, g, d):
            return copy_of(at(zz, x, c), g, x_s.at[d, e], at(z, shifted_x(d), c))

        def sib_send(e, zz, g, d):
            return copy_of(at(zz, shifted_x(d), c), g, sib_s.at[d, e], sib)

        def arrived(i, g):
            copy_of(i, g, sib_s.at[0, 0], sib).wait_recv()

        def send_on(e, zz, g):
            for go, copy in z_sends(e, zz, g):
                @pl.when(go)
                def _(copy=copy):
                    copy.start()
            for d in range(1, nx):
                x_send(e, zz, g, d).start()
            sib_send(e, zz, g, 0).start()

        def step_x(e):
            zz, g = event(e)
            for d in range(1, nx):
                arrived(at(zz, shifted_x(d), c), g)
                sib_send(e, zz, g, d).start()

        def step_sib(e):
            zz, g = event(e)
            for d in range(nx):
                arrived(at(zz, shifted_x(d), 1 - c), g)

            @pl.when(g == parts - 1)
            def _():
                consume(zz)

        for g in range(parts):
            prepare(g)
            send_on(g, z, g)
        if first is not None:
            first()

        def step(e):
            @pl.when(e < blocks)
            def _():
                zz, g = event(e)
                arrived(at(zz, x, c), g)
                send_on(e, zz, g)

            @pl.when(jnp.logical_and(e >= lag, e < blocks + lag))
            def _():
                step_x(e - lag)

            @pl.when(e >= lag + 2)
            def _():
                step_sib(e - lag - 2)

        loop(blocks + lag + 2 - parts, lambda i: step(i + parts))

        def settle(e):
            zz, g = event(e)
            for go, copy in z_sends(e, zz, g):
                @pl.when(go)
                def _(copy=copy):
                    copy.wait_send()
            for d in range(1, nx):
                x_send(e, zz, g, d).wait_send()
            for d in range(nx):
                sib_send(e, zz, g, d).wait_send()

        return lambda: loop(blocks, settle)


    def dec_send(q):
        return remote(
            dec_hbm.at[:, cols(2 * q + 1 - c)], cat.at[q, pl.ds(rows, rows), :],
            dsend.at[q], drecv.at[q], sib,
        )

    def dec_own(q):
        return pltpu.make_async_copy(
            dec_hbm.at[:, cols(2 * q + c)], cat.at[q, pl.ds(0, rows), :], load_sems.at[q]
        )

    def eye():
        i = lax.broadcasted_iota(jnp.int32, (rows, rows), 0)
        j = lax.broadcasted_iota(jnp.int32, (rows, rows), 1)
        return i == j

    def column(row):
        return jnp.sum(jnp.where(eye(), jnp.broadcast_to(row, (rows, rows)), 0.0), axis=1, keepdims=True)

    def row_of(col):
        return jnp.sum(jnp.where(eye(), jnp.broadcast_to(col, (rows, rows)), 0.0), axis=0, keepdims=True)

    slab = 2 * nx

    def start_rest():
        for q in range(nz * nx):
            dec_own(q).start()
            dec_send(q).start()
        pre_v[...] = jnp.zeros_like(pre_v)
        for load in loads:
            load.wait()

    def consume_acts(zz):
        acc = pre_v[...]
        for j in range(slab):
            i = zz * slab + j
            acc = acc + dot(enc_v[:, cols(i)], abuf[i], NT)
        pre_v[...] = acc

    def norms_and_counts():
        half = n // 2
        norms = []
        for m in range(2):
            def square(j, acc):
                w = dec_v[:, cols(m * half + j)].astype(f32)
                w = w * w
                for t in range(fb // 128):
                    acc = acc + w[:, t * 128:(t + 1) * 128]
                return acc
            acc = lax.fori_loop(0, half, square, jnp.zeros((rows, 128), f32))
            norms.append(jnp.sqrt(jnp.sum(acc, axis=1, keepdims=True) + norm_eps))
        active = lax.rem(mask_ref[...], 2).astype(f32)
        count = jnp.sum(active, axis=1, keepdims=True)
        lane = lax.broadcasted_iota(jnp.int32, (rows, 128), 1)
        coef_v[...] = jnp.where(
            lane == 0, sparsity_coef * count / norms[0],
            jnp.where(lane == 1, sparsity_coef * count / norms[1], norms[0] + norms[1]),
        )

    settle_acts = gather(abuf, a_up, a_x, a_sib, a_recv, consume_acts, lambda g: None, start_rest)

    active = lax.rem(mask_ref[...], 2).astype(f32)
    pre = pre_v[...] + column(encb_ref[...])
    feats = (active * pre).astype(bf16)
    feats2[pl.ds(0, rows), :] = feats
    fcopy = remote(
        feats2.at[pl.ds(0, rows), :], feats2.at[pl.ds(rows, rows), :], fsem.at[0], fsem.at[1], sib
    )
    fcopy.start()
    acts_copy = pltpu.make_async_copy(abuf, acts_out, out_sem.at[0])
    acts_copy.start()
    for q in range(nz * nx):
        dec_own(q).wait()
        dec_send(q).wait()
    fcopy.wait()

    both = feats2[...]

    def partial(q):
        return dot(both, cat[q], TN)

    piece = tokens // parts

    def lines(g):
        return pl.ds(pl.multiple_of(g * piece, piece), piece)

    def b_copy(k, zz, g, d):
        return remote(
            bsend.at[k * nx + d, lines(g), :], brecv.at[zz * nx + d, lines(g), :],
            b_s.at[k * nx + d, g], b_r.at[zz * nx + d, g], at(z, shifted_x(d), c),
        )

    def b_step(k, zz, g):
        for d in range(1, nx):
            @pl.when(g == 0)
            def _(d=d):
                bsend[k * nx + d] = partial(zz * nx + shifted_x(d)).astype(bf16)
            b_copy(k, zz, g, d).start()

    loop(events, lambda e: b_step(*farthest_first(e)))
    loop(parts, lambda g: b_step(0, z, g))
    for k in range(nz - 1, -1, -1):
        cpart[k] = partial(kth(k) * nx + x)
    settle_acts()
    norms_and_counts()

    def c_copies(k, zz, g):
        down_slot = zz + (nz - zz) * (zz == z - 1).astype(jnp.int32)
        return tuple(
            (go, remote(csend.at[k, lines(g), :], crecv.at[slot, lines(g), :], c_s.at[k, g], c_r.at[slot, g], device))
            for go, slot, device in ((zz > z, zz, at(z + 1, x, c)), (zz < z, down_slot, at(z - 1, x, c)))
        )

    def c_wait(slot, g):
        remote(csend.at[0, lines(g), :], crecv.at[slot, lines(g), :], c_s.at[0, g], c_r.at[slot, g], sib).wait_recv()

    def with_b(k, zz, g):
        part = cpart[k, lines(g), :]
        for d in range(1, nx):
            b_copy(k, zz, g, d).wait_recv()
            part = part + brecv[zz * nx + d, lines(g), :].astype(f32)
        return part

    def c_step(e):
        k, zz, g = farthest_first(e)
        part = with_b(k, zz, g)
        farther = jnp.logical_or(jnp.logical_and(zz > z, has_down), jnp.logical_and(zz < z, has_up))

        @pl.when(farther)
        def _():
            c_wait(zz, g)
            csend[k, lines(g), :] = (part + crecv[zz, lines(g), :].astype(f32)).astype(bf16)

        @pl.when(jnp.logical_not(farther))
        def _():
            csend[k, lines(g), :] = part.astype(bf16)

        for go, copy in c_copies(k, zz, g):
            @pl.when(go)
            def _(copy=copy):
                copy.start()

    loop(events, c_step)

    def prepare_error(g):
        actst[lines(g), :] = with_b(0, z, g) + decb_ref[...] - actst[lines(g), :]

        @pl.when(has_down)
        def _():
            c_wait(z, g)
            actst[lines(g), :] += crecv[z, lines(g), :].astype(f32)

        @pl.when(has_up)
        def _():
            c_wait(nz, g)
            actst[lines(g), :] += crecv[nz, lines(g), :].astype(f32)

        ebuf[me, lines(g), :] = actst[lines(g), :].astype(bf16)

    def gd_copy(zz):
        w = cols(zz * slab, slab * fb)
        return pltpu.make_async_copy(gd_v.at[:, w], gd_out.at[:, w], gd_sem.at[zz])

    def finish_sums():
        gdb_out[...] = scale * jnp.sum(ebuf[me].astype(f32), axis=0, keepdims=True)
        grec_v[...] = jnp.zeros_like(grec_v)

        def settle(k, zz, g):
            for d in range(1, nx):
                b_copy(k, zz, g, d).wait_send()

        def settle_c(e):
            k, zz, g = farthest_first(e)
            settle(k, zz, g)
            for go, copy in c_copies(k, zz, g):
                @pl.when(go)
                def _(copy=copy):
                    copy.wait_send()

        loop(events, settle_c)
        loop(parts, lambda g: settle(0, z, g))

    def consume_errors(zz):
        own = feats2[pl.ds(0, rows), :]

        def body(j, acc):
            i = zz * slab + j
            e = ebuf[i]
            w = dec_v[:, cols(i)]
            acc = acc + dot(w, e, NT)
            adjusted = (i >= n // 2).astype(f32)
            coef = coef_v[:, 0:1] + adjusted * (coef_v[:, 1:2] - coef_v[:, 0:1])
            gd_v[:, cols(i)] = (scale * (dot(own, e, NN) + coef * w.astype(f32))).astype(bf16)
            return acc

        grec_v[...] = lax.fori_loop(0, slab, body, grec_v[...])
        gd_copy(zz).start()

    settle_errors = gather(ebuf, e_up, e_x, e_sib, e_recv, consume_errors, prepare_error, finish_sums)

    grec = grec_v[...]
    active = lax.rem(mask_ref[...], 2).astype(f32)
    gpre = (active * grec).astype(bf16)
    gpre_out[...] = gpre
    window = (mask_ref[...] // 2).astype(f32)
    theta = window * (column(thr_ref[...]) * grec + sparsity_coef * coef_v[:, 2:3])
    gth_out[...] = row_of(-(scale / spread) * jnp.sum(theta, axis=1, keepdims=True))
    geb_out[...] = row_of(scale * jnp.sum(gpre.astype(f32), axis=1, keepdims=True))
    settle_errors()
    acts_copy.wait()
    for zz in range(nz):
        gd_copy(zz).wait()


def finish(scale, acts_ref, gpre_ref, gd_ref, geb_ref, gth_ref, gdb_ref, ge_o, gd_o, geb_o, gth_o, gdb_o):
    fb = acts_ref.shape[2]
    for j in range(acts_ref.shape[0]):
        ge_o[:, j * fb:(j + 1) * fb] = (scale * dot(gpre_ref[...], acts_ref[j], NN)).astype(bf16)
    gd_o[...] = gd_ref[...]
    geb_o[...] = geb_ref[...]
    gth_o[...] = gth_ref[...]
    gdb_o[...] = gdb_ref[...]


def per_device(lat, acts, mask, enc_weight, enc_bias, threshold, dec_weight, dec_bias):
    nz, nx = lat_shape(lat)
    n = lat
    rows, tokens = mask.shape
    fb = acts.shape[0]
    width = dec_weight.shape[1]
    scale = 1.0 / math.sqrt(tokens)
    vmem = pl.BlockSpec(memory_space=pltpu.VMEM)
    hbm = pl.BlockSpec(memory_space=pl.ANY)
    parts = 2
    dma = pltpu.SemaphoreType.DMA
    outs = pl.pallas_call(
        functools.partial(kernel, nz, nx, parts, scale),
        out_shape=(
            jax.ShapeDtypeStruct((n, tokens, fb), bf16),
            jax.ShapeDtypeStruct((rows, tokens), bf16),
            jax.ShapeDtypeStruct((1, rows), f32),
            jax.ShapeDtypeStruct((1, rows), f32),
            jax.ShapeDtypeStruct((rows, width), bf16),
            jax.ShapeDtypeStruct((1, fb), f32),
        ),
        in_specs=[hbm] * 7,
        out_specs=(hbm, vmem, vmem, vmem, hbm, vmem),
        scratch_shapes=[
            pltpu.VMEM((fb, tokens), bf16),
            pltpu.VMEM((rows, tokens), jnp.int32),
            pltpu.VMEM((1, rows), f32),
            pltpu.VMEM((1, rows), f32),
            pltpu.VMEM((1, fb), f32),
            pltpu.VMEM((rows, width), bf16),
            pltpu.VMEM((rows, width), bf16),
            pltpu.VMEM((nz * nx, 2 * rows, fb), bf16),
            pltpu.VMEM((n, tokens, fb), bf16),
            pltpu.VMEM((n, tokens, fb), bf16),
            pltpu.VMEM((2 * rows, tokens), bf16),
            pltpu.VMEM((rows, tokens), f32),
            pltpu.VMEM((rows, tokens), f32),
            pltpu.VMEM((rows, 128), f32),
            pltpu.VMEM((nz * nx, tokens, fb), bf16),
            pltpu.VMEM((nz * nx, tokens, fb), bf16),
            pltpu.VMEM((nz, tokens, fb), bf16),
            pltpu.VMEM((nz + 1, tokens, fb), bf16),
            pltpu.VMEM((nz, tokens, fb), f32),
            pltpu.VMEM((rows, width), bf16),
            pltpu.VMEM((tokens, fb), f32),
            dma((7 + nz * nx,)), dma((nz * nx,)), dma((nz * nx,)), dma((2,)),
            dma((2, nz * parts)), dma((nx, nz * parts)), dma((nx, nz * parts)), dma((n, parts)),
            dma((2, nz * parts)), dma((nx, nz * parts)), dma((nx, nz * parts)), dma((n, parts)),
            dma((nz * nx, parts)), dma((nz * nx, parts)), dma((nz, parts)), dma((nz + 1, parts)),
            dma((nz,)), dma((1,)),
        ],
        compiler_params=pltpu.CompilerParams(
            collective_id=0, has_side_effects=True, vmem_limit_bytes=56 * 1024 * 1024
        ),
        name="crosscoder",
    )(
        acts, mask, enc_bias.reshape(1, rows), threshold.reshape(1, rows),
        dec_bias.reshape(1, fb), enc_weight, dec_weight,
    )
    all_acts, gpre, geb, gth, gd, gdb = outs
    steps = 8
    block = width // steps
    held = lambda shape: pl.BlockSpec(shape, lambda i: (0, 0))
    across = pl.BlockSpec((rows, block), lambda i: (0, i))
    small = [held((1, rows)), held((1, rows)), held((1, fb))]
    ge, gd, geb, gth, gdb = pl.pallas_call(
        functools.partial(finish, scale),
        grid=(steps,),
        out_shape=(
            jax.ShapeDtypeStruct((rows, width), bf16),
            jax.ShapeDtypeStruct((rows, width), bf16),
            jax.ShapeDtypeStruct((1, rows), f32),
            jax.ShapeDtypeStruct((1, rows), f32),
            jax.ShapeDtypeStruct((1, fb), f32),
        ),
        in_specs=[pl.BlockSpec((n // steps, tokens, fb), lambda i: (i, 0, 0)), held((rows, tokens)), across] + small,
        out_specs=[across, across] + small,
        compiler_params=pltpu.CompilerParams(vmem_limit_bytes=60 * 1024 * 1024),
        name="last_products",
    )(all_acts, gpre, gd, geb, gth, gdb)
    return ge, geb.reshape(rows), gth.reshape(rows), gd, gdb.reshape(fb)


def solution(mesh):
    wide, flat = P(("groups", "lat"), None), P(("groups", "lat"))
    return jax.shard_map(
        functools.partial(per_device, mesh.shape["lat"]), mesh=mesh,
        in_specs=(wide, wide, wide, flat, flat, wide, flat),
        out_specs=(wide, flat, flat, wide, flat), check_vma=False,
    )
```

```python
import functools
import math

import jax
import jax.numpy as jnp
from jax import lax
from jax.experimental import pallas as pl
from jax.experimental.pallas import tpu as pltpu
from jax.sharding import PartitionSpec as P

sparsity_coef = 0.1
spread = 0.1
norm_eps = 1e-06

MESH = pl.DeviceIdType.MESH
f32 = jnp.float32
bf16 = jnp.bfloat16


def lat_shape(lat):
    chips = lat // 2
    nx = 1
    while (2 * nx) ** 3 <= chips:
        nx *= 2
    return chips // nx, nx


def dot(a, b, dims):
    return lax.dot_general(a, b, (dims, ((), ())), preferred_element_type=f32)


NN = ((1,), (0,))
NT = ((1,), (1,))
TN = ((0,), (0,))


def kernel(
    nz, nx, parts, scale,
    acts_hbm, mask_hbm, encb_hbm, thr_hbm, decb_hbm, enc_hbm, dec_hbm,
    acts_out, gpre_out, geb_out, gth_out, gd_out, gdb_out,
    acts_ref, mask_ref, encb_ref, thr_ref, decb_ref, enc_v, dec_v, cat, abuf, ebuf, feats2, pre_v, grec_v, coef_v,
    bsend, brecv, csend, crecv, cpart, gd_v, actst,
    load_sems, dsend, drecv, fsem,
    a_up, a_x, a_sib, a_recv, e_up, e_x, e_sib, e_recv,
    b_s, b_r, c_s, c_r, gd_sem, out_sem,
):
    n = 2 * nz * nx
    rows = mask_hbm.shape[0]
    fb, tokens = acts_hbm.shape
    me = lax.axis_index("lat")
    c = lax.rem(me, 2)
    x = lax.rem(me // 2, nx)
    z = me // (2 * nx)
    sib = me + 1 - 2 * c

    def at(zz, xx, cc):
        return (zz * nx + xx) * 2 + cc

    def shifted_x(d):
        return lax.rem(x + d, nx)

    def cols(i, width=fb):
        return pl.ds(pl.multiple_of(i * fb, 128), width)

    short = jnp.minimum(z, nz - 1 - z)
    upper = (2 * z < nz - 1).astype(jnp.int32)
    events = (nz - 1) * parts

    def place(paired, p, w, k, g):
        paired = paired.astype(jnp.int32)
        zz = paired * (z + (p + 1) * (2 * (w % 2) - 1)) + (1 - paired) * (z + (2 * upper - 1) * (k - short))
        k = paired * (2 * p + 1 + w % 2) + (1 - paired) * k
        g = paired * (w // 2) + (1 - paired) * g
        return k, zz, g

    def nearest_first(e, parts=3):
        p, w = e // (2 * parts), e % (2 * parts)
        return place(p < short, p, w, 1 + e // parts, e % parts)

    def farthest_first(e):
        alone = (nz - 1 - 2 * short) * parts
        rest = jnp.maximum(e - alone, 0)
        p, w = short - 1 - rest // (2 * parts), rest % (2 * parts)
        return place(e >= alone, p, w, nz - 1 - e // parts, e % parts)

    def kth(k):
        if k == 0:
            return z
        paired = z - (k + 1) // 2 if k % 2 else z + k // 2
        alone = z + (2 * upper - 1) * (k - short)
        both = (k <= 2 * short).astype(jnp.int32)
        return both * paired + (1 - both) * alone

    def loop(count, body):
        def step(i, carry):
            body(i)
            return carry
        lax.fori_loop(0, count, step, 0)

    barrier = pltpu.get_barrier_semaphore()

    def greet(device):
        pl.semaphore_signal(barrier, inc=1, device_id={"lat": device}, device_id_type=MESH)

    has_down = z >= 1
    has_up = z <= nz - 2

    @pl.when(has_down)
    def _():
        greet(at(z - 1, x, c))

    @pl.when(has_up)
    def _():
        greet(at(z + 1, x, c))

    for d in range(1, nx):
        greet(at(z, shifted_x(d), c))
    greet(sib)

    acts_load, *loads = [
        pltpu.make_async_copy(src, dst, load_sems.at[nz * nx + i])
        for i, (src, dst) in enumerate((
            (acts_hbm, acts_ref), (mask_hbm, mask_ref), (encb_hbm, encb_ref), (thr_hbm, thr_ref),
            (decb_hbm, decb_ref), (enc_hbm, enc_v), (dec_hbm, dec_v),
        ))
    ]
    acts_load.start()
    for load in loads:
        load.start()
    acts_load.wait()
    actst[...] = acts_ref[...].astype(f32).T
    abuf[me] = actst[...].astype(bf16)

    pl.semaphore_wait(barrier, nx + has_down.astype(jnp.int32) + has_up.astype(jnp.int32))

    def remote(src, dst, send, recv, device):
        return pltpu.make_async_remote_copy(
            src_ref=src, dst_ref=dst, send_sem=send, recv_sem=recv,
            device_id={"lat": device}, device_id_type=MESH,
        )

    def gather(buf, up_s, x_s, sib_s, recv, consume, prepare, first):
        height = buf.shape[1]
        thin, half = height // 8, height // 2
        spans = ((thin, half - thin), (half, height - half), (0, thin))
        pieces, wide = len(spans), len(spans) - 1
        blocks, lag = nz * pieces, 2 * pieces

        def copy_of(i, g, send, device):
            view = buf.at[i, pl.ds(*spans[g]), :]
            return remote(view, view, send, recv.at[i, g], device)

        def event(e):
            k, zz, g = nearest_first(jnp.maximum(e - pieces, 0))
            own = (e < pieces).astype(jnp.int32)
            return zz + own * (z - zz), g + own * (e - g)

        def by_piece(g, act):
            for s in range(pieces):
                @pl.when(g == s)
                def _(s=s):
                    act(s)

        def z_sends(e, zz, g, d):
            i = at(zz, shifted_x(d), c)
            go_up = jnp.logical_and(zz <= z, has_up)
            go_down = jnp.logical_and(zz >= z, has_down)
            return (
                (go_up, copy_of(i, g, up_s.at[0, d, e], at(z + 1, x, c))),
                (go_down, copy_of(i, g, up_s.at[1, d, e], at(z - 1, x, c))),
            )

        def x_send(e, zz, g, d):
            return copy_of(at(zz, x, c), g, x_s.at[d, e], at(z, shifted_x(d), c))

        def sib_send(e, zz, g, d):
            return copy_of(at(zz, shifted_x(d), c), g, sib_s.at[d, e], sib)

        def arrived(i, g):
            copy_of(i, g, sib_s.at[0, 0], sib).wait_recv()

        def along(e, zz, g, d):
            for go, copy in z_sends(e, zz, g, d):
                @pl.when(go)
                def _(copy=copy):
                    copy.start()

        def across(e, zz, g):
            for d in range(1, nx):
                x_send(e, zz, g, d).start()

        def step_z(e):
            zz, piece = event(e)

            def act(g):
                for d in range(nx if g == wide else 1):
                    arrived(at(zz, shifted_x(d), c), g)
                    along(e, zz, g, d)
                    if g != wide:
                        across(e, zz, g)
                    sib_send(e, zz, g, d).start()

            by_piece(piece, act)

        def step_x(e):
            zz, piece = event(e)

            def act(g):
                for d in range(1, nx if g != wide else 1):
                    arrived(at(zz, shifted_x(d), c), g)
                    sib_send(e, zz, g, d).start()

            by_piece(piece, act)

        def step_sib(e):
            zz, piece = event(e)

            def act(g):
                for d in range(nx):
                    arrived(at(zz, shifted_x(d), 1 - c), g)

            by_piece(piece, act)

            @pl.when(piece == pieces - 1)
            def _():
                consume(zz)

        for g in (wide, 0, 1):
            prepare(g)
            across(g, z, g)
            along(g, z, g, 0)
            sib_send(g, z, g, 0).start()
        for d in range(1, nx):
            arrived(at(z, shifted_x(d), c), wide)
            along(wide, z, wide, d)
            sib_send(wide, z, wide, d).start()
        first()

        def step(e):
            @pl.when(e < blocks)
            def _():
                step_z(e)

            @pl.when(jnp.logical_and(e >= lag, e < blocks + lag))
            def _():
                step_x(e - lag)

            @pl.when(e >= lag + 1)
            def _():
                step_sib(e - lag - 1)

        loop(blocks + lag + 1 - pieces, lambda i: step(i + pieces))

        def settle(e):
            zz, piece = event(e)

            def act(g):
                for d in range(nx if g == wide else 1):
                    for go, copy in z_sends(e, zz, g, d):
                        @pl.when(go)
                        def _(copy=copy):
                            copy.wait_send()
                for d in range(nx):
                    sib_send(e, zz, g, d).wait_send()
                if g != wide:
                    for d in range(1, nx):
                        x_send(e, zz, g, d).wait_send()

            by_piece(piece, act)

        def settle_all():
            for d in range(1, nx):
                x_send(wide, z, wide, d).wait_send()
            loop(blocks, settle)

        return settle_all


    def dec_send(q):
        return remote(
            dec_hbm.at[:, cols(2 * q + 1 - c)], cat.at[q, pl.ds(rows, rows), :],
            dsend.at[q], drecv.at[q], sib,
        )

    def dec_own(q):
        return pltpu.make_async_copy(
            dec_hbm.at[:, cols(2 * q + c)], cat.at[q, pl.ds(0, rows), :], load_sems.at[q]
        )

    def eye():
        i = lax.broadcasted_iota(jnp.int32, (rows, rows), 0)
        j = lax.broadcasted_iota(jnp.int32, (rows, rows), 1)
        return i == j

    def column(row):
        return jnp.sum(jnp.where(eye(), jnp.broadcast_to(row, (rows, rows)), 0.0), axis=1, keepdims=True)

    def row_of(col):
        return jnp.sum(jnp.where(eye(), jnp.broadcast_to(col, (rows, rows)), 0.0), axis=0, keepdims=True)

    slab = 2 * nx

    def start_rest():
        for q in range(nz * nx):
            dec_own(q).start()
            dec_send(q).start()
        pre_v[...] = jnp.zeros_like(pre_v)
        for load in loads:
            load.wait()

    def consume_acts(zz):
        acc = pre_v[...]
        for j in range(slab):
            i = zz * slab + j
            acc = acc + dot(enc_v[:, cols(i)], abuf[i], NT)
        pre_v[...] = acc

    def norms_and_counts():
        half = n // 2
        norms = []
        for m in range(2):
            def square(j, acc):
                w = dec_v[:, cols(m * half + j)].astype(f32)
                w = w * w
                for t in range(fb // 128):
                    acc = acc + w[:, t * 128:(t + 1) * 128]
                return acc
            acc = lax.fori_loop(0, half, square, jnp.zeros((rows, 128), f32))
            norms.append(jnp.sqrt(jnp.sum(acc, axis=1, keepdims=True) + norm_eps))
        active = lax.rem(mask_ref[...], 2).astype(f32)
        count = jnp.sum(active, axis=1, keepdims=True)
        lane = lax.broadcasted_iota(jnp.int32, (rows, 128), 1)
        coef_v[...] = jnp.where(
            lane == 0, sparsity_coef * count / norms[0],
            jnp.where(lane == 1, sparsity_coef * count / norms[1], norms[0] + norms[1]),
        )

    settle_acts = gather(abuf, a_up, a_x, a_sib, a_recv, consume_acts, lambda g: None, start_rest)

    active = lax.rem(mask_ref[...], 2).astype(f32)
    pre = pre_v[...] + column(encb_ref[...])
    feats = (active * pre).astype(bf16)
    feats2[pl.ds(0, rows), :] = feats
    fcopy = remote(
        feats2.at[pl.ds(0, rows), :], feats2.at[pl.ds(rows, rows), :], fsem.at[0], fsem.at[1], sib
    )
    fcopy.start()
    acts_copy = pltpu.make_async_copy(abuf, acts_out, out_sem.at[0])
    acts_copy.start()
    for q in range(nz * nx):
        dec_own(q).wait()
        dec_send(q).wait()
    fcopy.wait()

    both = feats2[...]

    def partial(q):
        return dot(both, cat[q], TN)

    piece = tokens // parts

    def lines(g):
        return pl.ds(pl.multiple_of(g * piece, piece), piece)

    def b_copy(k, zz, g, d):
        return remote(
            bsend.at[k * nx + d, lines(g), :], brecv.at[zz * nx + d, lines(g), :],
            b_s.at[k * nx + d, g], b_r.at[zz * nx + d, g], at(z, shifted_x(d), c),
        )

    def b_step(k, zz, g):
        for d in range(1, nx):
            @pl.when(g == 0)
            def _(d=d):
                bsend[k * nx + d] = partial(zz * nx + shifted_x(d)).astype(bf16)
            b_copy(k, zz, g, d).start()

    loop(events, lambda e: b_step(*farthest_first(e)))
    loop(parts, lambda g: b_step(0, z, g))
    for k in range(nz - 1, -1, -1):
        cpart[k] = partial(kth(k) * nx + x)
    settle_acts()
    norms_and_counts()

    def c_copies(k, zz, g):
        down_slot = zz + (nz - zz) * (zz == z - 1).astype(jnp.int32)
        return tuple(
            (go, remote(csend.at[k, lines(g), :], crecv.at[slot, lines(g), :], c_s.at[k, g], c_r.at[slot, g], device))
            for go, slot, device in ((zz > z, zz, at(z + 1, x, c)), (zz < z, down_slot, at(z - 1, x, c)))
        )

    def c_wait(slot, g):
        remote(csend.at[0, lines(g), :], crecv.at[slot, lines(g), :], c_s.at[0, g], c_r.at[slot, g], sib).wait_recv()

    def with_b(k, zz, g):
        part = cpart[k, lines(g), :]
        for d in range(1, nx):
            b_copy(k, zz, g, d).wait_recv()
            part = part + brecv[zz * nx + d, lines(g), :].astype(f32)
        return part

    def c_step(e):
        k, zz, g = farthest_first(e)
        part = with_b(k, zz, g)
        farther = jnp.logical_or(jnp.logical_and(zz > z, has_down), jnp.logical_and(zz < z, has_up))

        @pl.when(farther)
        def _():
            c_wait(zz, g)
            csend[k, lines(g), :] = (part + crecv[zz, lines(g), :].astype(f32)).astype(bf16)

        @pl.when(jnp.logical_not(farther))
        def _():
            csend[k, lines(g), :] = part.astype(bf16)

        for go, copy in c_copies(k, zz, g):
            @pl.when(go)
            def _(copy=copy):
                copy.start()

    loop(events, c_step)

    def prepare_error(piece):
        if piece == 0:
            return
        g = 2 - piece
        actst[lines(g), :] = with_b(0, z, g) + decb_ref[...] - actst[lines(g), :]

        @pl.when(has_down)
        def _():
            c_wait(z, g)
            actst[lines(g), :] += crecv[z, lines(g), :].astype(f32)

        @pl.when(has_up)
        def _():
            c_wait(nz, g)
            actst[lines(g), :] += crecv[nz, lines(g), :].astype(f32)

        ebuf[me, lines(g), :] = actst[lines(g), :].astype(bf16)

    def gd_copy(zz):
        w = cols(zz * slab, slab * fb)
        return pltpu.make_async_copy(gd_v.at[:, w], gd_out.at[:, w], gd_sem.at[zz])

    def finish_sums():
        gdb_out[...] = scale * jnp.sum(ebuf[me].astype(f32), axis=0, keepdims=True)
        grec_v[...] = jnp.zeros_like(grec_v)

        def settle(k, zz, g):
            for d in range(1, nx):
                b_copy(k, zz, g, d).wait_send()

        def settle_c(e):
            k, zz, g = farthest_first(e)
            settle(k, zz, g)
            for go, copy in c_copies(k, zz, g):
                @pl.when(go)
                def _(copy=copy):
                    copy.wait_send()

        loop(events, settle_c)
        loop(parts, lambda g: settle(0, z, g))

    def consume_errors(zz):
        own = feats2[pl.ds(0, rows), :]

        def body(j, acc):
            i = zz * slab + j
            e = ebuf[i]
            w = dec_v[:, cols(i)]
            acc = acc + dot(w, e, NT)
            adjusted = (i >= n // 2).astype(f32)
            coef = coef_v[:, 0:1] + adjusted * (coef_v[:, 1:2] - coef_v[:, 0:1])
            gd_v[:, cols(i)] = (scale * (dot(own, e, NN) + coef * w.astype(f32))).astype(bf16)
            return acc

        grec_v[...] = lax.fori_loop(0, slab, body, grec_v[...])
        gd_copy(zz).start()

    settle_errors = gather(ebuf, e_up, e_x, e_sib, e_recv, consume_errors, prepare_error, finish_sums)

    grec = grec_v[...]
    active = lax.rem(mask_ref[...], 2).astype(f32)
    gpre = (active * grec).astype(bf16)
    gpre_out[...] = gpre
    window = (mask_ref[...] // 2).astype(f32)
    theta = window * (column(thr_ref[...]) * grec + sparsity_coef * coef_v[:, 2:3])
    gth_out[...] = row_of(-(scale / spread) * jnp.sum(theta, axis=1, keepdims=True))
    geb_out[...] = row_of(scale * jnp.sum(gpre.astype(f32), axis=1, keepdims=True))
    settle_errors()
    acts_copy.wait()
    for zz in range(nz):
        gd_copy(zz).wait()


def finish(
    scale, acts_in, gpre_ref, gd_in, geb_ref, gth_ref, gdb_ref, ge_out, gd_out, geb_o, gth_o, gdb_o,
    acts_v, gd_v, ge_v, gd_r, gd_w, acts_r, ge_w,
):
    steps, strips = acts_r.shape[0], gd_r.shape[0]
    per, fb = acts_v.shape[0] // steps, acts_v.shape[2]
    tall = gd_v.shape[0] // strips

    def gd_read(i):
        rows = pl.ds(i * tall, tall)
        return pltpu.make_async_copy(gd_in.at[rows, :], gd_v.at[rows, :], gd_r.at[i])

    def gd_write(i):
        rows = pl.ds(i * tall, tall)
        return pltpu.make_async_copy(gd_v.at[rows, :], gd_out.at[rows, :], gd_w.at[i])

    def acts_read(i):
        some = pl.ds(i * per, per)
        return pltpu.make_async_copy(acts_in.at[some], acts_v.at[some], acts_r.at[i])

    def ge_write(i):
        w = pl.ds(i * per * fb, per * fb)
        return pltpu.make_async_copy(ge_v.at[:, w], ge_out.at[:, w], ge_w.at[i])

    for i in range(max(steps, strips)):
        if i < strips:
            gd_read(i).start()
        if i < steps:
            acts_read(i).start()
    geb_o[...] = geb_ref[...]
    gth_o[...] = gth_ref[...]
    gdb_o[...] = gdb_ref[...]
    for i in range(max(steps, strips)):
        if i < strips:
            gd_read(i).wait()
            gd_write(i).start()
        if i < steps:
            acts_read(i).wait()
            for j in range(i * per, (i + 1) * per):
                ge_v[:, j * fb:(j + 1) * fb] = (scale * dot(gpre_ref[...], acts_v[j], NN)).astype(bf16)
            ge_write(i).start()
    for i in range(strips):
        gd_write(i).wait()
    for i in range(steps):
        ge_write(i).wait()


def per_device(lat, acts, mask, enc_weight, enc_bias, threshold, dec_weight, dec_bias):
    nz, nx = lat_shape(lat)
    n = lat
    rows, tokens = mask.shape
    fb = acts.shape[0]
    width = dec_weight.shape[1]
    scale = 1.0 / math.sqrt(tokens)
    vmem = pl.BlockSpec(memory_space=pltpu.VMEM)
    hbm = pl.BlockSpec(memory_space=pl.ANY)
    parts = 2
    dma = pltpu.SemaphoreType.DMA
    outs = pl.pallas_call(
        functools.partial(kernel, nz, nx, parts, scale),
        out_shape=(
            jax.ShapeDtypeStruct((n, tokens, fb), bf16),
            jax.ShapeDtypeStruct((rows, tokens), bf16),
            jax.ShapeDtypeStruct((1, rows), f32),
            jax.ShapeDtypeStruct((1, rows), f32),
            jax.ShapeDtypeStruct((rows, width), bf16),
            jax.ShapeDtypeStruct((1, fb), f32),
        ),
        in_specs=[hbm] * 7,
        out_specs=(hbm, vmem, vmem, vmem, hbm, vmem),
        scratch_shapes=[
            pltpu.VMEM((fb, tokens), bf16),
            pltpu.VMEM((rows, tokens), jnp.int32),
            pltpu.VMEM((1, rows), f32),
            pltpu.VMEM((1, rows), f32),
            pltpu.VMEM((1, fb), f32),
            pltpu.VMEM((rows, width), bf16),
            pltpu.VMEM((rows, width), bf16),
            pltpu.VMEM((nz * nx, 2 * rows, fb), bf16),
            pltpu.VMEM((n, tokens, fb), bf16),
            pltpu.VMEM((n, tokens, fb), bf16),
            pltpu.VMEM((2 * rows, tokens), bf16),
            pltpu.VMEM((rows, tokens), f32),
            pltpu.VMEM((rows, tokens), f32),
            pltpu.VMEM((rows, 128), f32),
            pltpu.VMEM((nz * nx, tokens, fb), bf16),
            pltpu.VMEM((nz * nx, tokens, fb), bf16),
            pltpu.VMEM((nz, tokens, fb), bf16),
            pltpu.VMEM((nz + 1, tokens, fb), bf16),
            pltpu.VMEM((nz, tokens, fb), f32),
            pltpu.VMEM((rows, width), bf16),
            pltpu.VMEM((tokens, fb), f32),
            dma((7 + nz * nx,)), dma((nz * nx,)), dma((nz * nx,)), dma((2,)),
            dma((2, nx, nz * 3)), dma((nx, nz * 3)), dma((nx, nz * 3)), dma((n, 3)),
            dma((2, nx, nz * 3)), dma((nx, nz * 3)), dma((nx, nz * 3)), dma((n, 3)),
            dma((nz * nx, parts)), dma((nz * nx, parts)), dma((nz, parts)), dma((nz + 1, parts)),
            dma((nz,)), dma((1,)),
        ],
        compiler_params=pltpu.CompilerParams(
            collective_id=0, has_side_effects=True, vmem_limit_bytes=56 * 1024 * 1024
        ),
        name="crosscoder",
    )(
        acts, mask, enc_bias.reshape(1, rows), threshold.reshape(1, rows),
        dec_bias.reshape(1, fb), enc_weight, dec_weight,
    )
    all_acts, gpre, geb, gth, gd, gdb = outs
    steps, strips = 8, rows // 16
    ge, gd, geb, gth, gdb = pl.pallas_call(
        functools.partial(finish, scale),
        out_shape=(
            jax.ShapeDtypeStruct((rows, width), bf16),
            jax.ShapeDtypeStruct((rows, width), bf16),
            jax.ShapeDtypeStruct((1, rows), f32),
            jax.ShapeDtypeStruct((1, rows), f32),
            jax.ShapeDtypeStruct((1, fb), f32),
        ),
        in_specs=[hbm, vmem, hbm] + [vmem] * 3,
        out_specs=(hbm, hbm, vmem, vmem, vmem),
        scratch_shapes=[
            pltpu.VMEM((n, tokens, fb), bf16), pltpu.VMEM((rows, width), bf16), pltpu.VMEM((rows, width), bf16),
            dma((strips,)), dma((strips,)), dma((steps,)), dma((steps,)),
        ],
        compiler_params=pltpu.CompilerParams(vmem_limit_bytes=60 * 1024 * 1024),
        name="last_products",
    )(all_acts, gpre, gd, geb, gth, gdb)
    return ge, geb.reshape(rows), gth.reshape(rows), gd, gdb.reshape(fb)


def solution(mesh):
    wide, flat = P(("groups", "lat"), None), P(("groups", "lat"))
    return jax.shard_map(
        functools.partial(per_device, mesh.shape["lat"]), mesh=mesh,
        in_specs=(wide, wide, wide, flat, flat, wide, flat),
        out_specs=(wide, flat, flat, wide, flat), check_vma=False,
    )
```

```python
import functools
import math

import jax
import jax.numpy as jnp
from jax import lax
from jax.experimental import pallas as pl
from jax.experimental.pallas import tpu as pltpu
from jax.sharding import PartitionSpec as P

sparsity_coef = 0.1
spread = 0.1
norm_eps = 1e-06

MESH = pl.DeviceIdType.MESH
f32 = jnp.float32
bf16 = jnp.bfloat16


def lat_shape(lat):
    chips = lat // 2
    nx = 1
    while (2 * nx) ** 3 <= chips:
        nx *= 2
    return chips // nx, nx


def dot(a, b, dims):
    return lax.dot_general(a, b, (dims, ((), ())), preferred_element_type=f32)


NN = ((1,), (0,))
NT = ((1,), (1,))
TN = ((0,), (0,))


def kernel(
    nz, nx, parts, scale,
    acts_hbm, mask_hbm, encb_hbm, thr_hbm, decb_hbm, enc_hbm, dec_hbm,
    acts_out, gpre_out, geb_out, gth_out, gd_out, gdb_out,
    acts_ref, mask_ref, encb_ref, thr_ref, decb_ref, enc_v, dec_v, cat, abuf, ebuf, feats2, pre_v, grec_v, coef_v,
    bsend, brecv, csend, crecv, cpart, gd_v, actst,
    load_sems, dsend, drecv, fsem,
    a_up, a_x, a_sib, a_recv, e_up, e_x, e_sib, e_recv,
    b_s, b_r, c_s, c_r, gd_sem, out_sem,
):
    n = 2 * nz * nx
    rows = mask_hbm.shape[0]
    fb, tokens = acts_hbm.shape
    me = lax.axis_index("lat")
    c = lax.rem(me, 2)
    x = lax.rem(me // 2, nx)
    z = me // (2 * nx)
    sib = me + 1 - 2 * c

    def at(zz, xx, cc):
        return (zz * nx + xx) * 2 + cc

    def shifted_x(d):
        return lax.rem(x + d, nx)

    def cols(i, width=fb):
        return pl.ds(pl.multiple_of(i * fb, 128), width)

    short = jnp.minimum(z, nz - 1 - z)
    upper = (2 * z < nz - 1).astype(jnp.int32)
    events = (nz - 1) * parts

    def place(paired, p, w, k, g):
        paired = paired.astype(jnp.int32)
        zz = paired * (z + (p + 1) * (2 * (w % 2) - 1)) + (1 - paired) * (z + (2 * upper - 1) * (k - short))
        k = paired * (2 * p + 1 + w % 2) + (1 - paired) * k
        g = paired * (w // 2) + (1 - paired) * g
        return k, zz, g

    def nearest_first(e, parts=3):
        p, w = e // (2 * parts), e % (2 * parts)
        return place(p < short, p, w, 1 + e // parts, e % parts)

    def farthest_first(e):
        alone = (nz - 1 - 2 * short) * parts
        rest = jnp.maximum(e - alone, 0)
        p, w = short - 1 - rest // (2 * parts), rest % (2 * parts)
        return place(e >= alone, p, w, nz - 1 - e // parts, e % parts)

    def kth(k):
        if k == 0:
            return z
        paired = z - (k + 1) // 2 if k % 2 else z + k // 2
        alone = z + (2 * upper - 1) * (k - short)
        both = (k <= 2 * short).astype(jnp.int32)
        return both * paired + (1 - both) * alone

    def loop(count, body):
        def step(i, carry):
            body(i)
            return carry
        lax.fori_loop(0, count, step, 0)

    barrier = pltpu.get_barrier_semaphore()

    def greet(device):
        pl.semaphore_signal(barrier, inc=1, device_id={"lat": device}, device_id_type=MESH)

    has_down = z >= 1
    has_up = z <= nz - 2

    @pl.when(has_down)
    def _():
        greet(at(z - 1, x, c))

    @pl.when(has_up)
    def _():
        greet(at(z + 1, x, c))

    for d in range(1, nx):
        greet(at(z, shifted_x(d), c))
    greet(sib)

    acts_load, *loads = [
        pltpu.make_async_copy(src, dst, load_sems.at[nz * nx + i])
        for i, (src, dst) in enumerate((
            (acts_hbm, acts_ref), (mask_hbm, mask_ref), (encb_hbm, encb_ref), (thr_hbm, thr_ref),
            (decb_hbm, decb_ref), (enc_hbm, enc_v), (dec_hbm, dec_v),
        ))
    ]
    acts_load.start()
    for load in loads:
        load.start()
    acts_load.wait()
    actst[...] = acts_ref[...].astype(f32).T
    abuf[me] = actst[...].astype(bf16)

    pl.semaphore_wait(barrier, nx + has_down.astype(jnp.int32) + has_up.astype(jnp.int32))

    def remote(src, dst, send, recv, device):
        return pltpu.make_async_remote_copy(
            src_ref=src, dst_ref=dst, send_sem=send, recv_sem=recv,
            device_id={"lat": device}, device_id_type=MESH,
        )

    def gather(buf, up_s, x_s, sib_s, recv, consume, prepare, first):
        height = buf.shape[1]
        thin, half = height // 8, height // 2
        spans = ((thin, half - thin), (half, height - half), (0, thin))
        pieces, wide = len(spans), len(spans) - 1
        blocks, lag = nz * pieces, 2 * pieces

        def copy_of(i, g, send, device):
            view = buf.at[i, pl.ds(*spans[g]), :]
            return remote(view, view, send, recv.at[i, g], device)

        def event(e):
            k, zz, g = nearest_first(jnp.maximum(e - pieces, 0))
            own = (e < pieces).astype(jnp.int32)
            return zz + own * (z - zz), g + own * (e - g)

        def by_piece(g, act):
            for s in range(pieces):
                @pl.when(g == s)
                def _(s=s):
                    act(s)

        def z_sends(e, zz, g, d):
            i = at(zz, shifted_x(d), c)
            go_up = jnp.logical_and(zz <= z, has_up)
            go_down = jnp.logical_and(zz >= z, has_down)
            return (
                (go_up, copy_of(i, g, up_s.at[0, d, e], at(z + 1, x, c))),
                (go_down, copy_of(i, g, up_s.at[1, d, e], at(z - 1, x, c))),
            )

        def x_send(e, zz, g, d):
            return copy_of(at(zz, x, c), g, x_s.at[d, e], at(z, shifted_x(d), c))

        def sib_send(e, zz, g, d):
            return copy_of(at(zz, shifted_x(d), c), g, sib_s.at[d, e], sib)

        def arrived(i, g):
            copy_of(i, g, sib_s.at[0, 0], sib).wait_recv()

        def along(e, zz, g, d):
            for go, copy in z_sends(e, zz, g, d):
                @pl.when(go)
                def _(copy=copy):
                    copy.start()

        def across(e, zz, g):
            for d in range(1, nx):
                x_send(e, zz, g, d).start()

        def step_z(e):
            zz, piece = event(e)

            def act(g):
                for d in range(nx if g == wide else 1):
                    arrived(at(zz, shifted_x(d), c), g)
                    along(e, zz, g, d)
                    if g != wide:
                        across(e, zz, g)
                    sib_send(e, zz, g, d).start()

            by_piece(piece, act)

        def step_x(e):
            zz, piece = event(e)

            def act(g):
                for d in range(1, nx if g != wide else 1):
                    arrived(at(zz, shifted_x(d), c), g)
                    sib_send(e, zz, g, d).start()

            by_piece(piece, act)

        def step_sib(e):
            zz, piece = event(e)

            def act(g):
                for d in range(nx):
                    arrived(at(zz, shifted_x(d), 1 - c), g)

            by_piece(piece, act)

            @pl.when(piece == pieces - 1)
            def _():
                consume(zz)

        for g in (wide, 0, 1):
            prepare(g)
            across(g, z, g)
            along(g, z, g, 0)
            sib_send(g, z, g, 0).start()
        for d in range(1, nx):
            arrived(at(z, shifted_x(d), c), wide)
            along(wide, z, wide, d)
            sib_send(wide, z, wide, d).start()
        first()

        def step(e):
            @pl.when(e < blocks)
            def _():
                step_z(e)

            @pl.when(jnp.logical_and(e >= lag, e < blocks + lag))
            def _():
                step_x(e - lag)

            @pl.when(e >= lag + 1)
            def _():
                step_sib(e - lag - 1)

        loop(blocks + lag + 1 - pieces, lambda i: step(i + pieces))

        def settle(e):
            zz, piece = event(e)

            def act(g):
                for d in range(nx if g == wide else 1):
                    for go, copy in z_sends(e, zz, g, d):
                        @pl.when(go)
                        def _(copy=copy):
                            copy.wait_send()
                for d in range(nx):
                    sib_send(e, zz, g, d).wait_send()
                if g != wide:
                    for d in range(1, nx):
                        x_send(e, zz, g, d).wait_send()

            by_piece(piece, act)

        def settle_all():
            for d in range(1, nx):
                x_send(wide, z, wide, d).wait_send()
            loop(blocks, settle)

        return settle_all


    def dec_send(q):
        return remote(
            dec_hbm.at[:, cols(2 * q + 1 - c)], cat.at[q, pl.ds(rows, rows), :],
            dsend.at[q], drecv.at[q], sib,
        )

    def dec_own(q):
        return pltpu.make_async_copy(
            dec_hbm.at[:, cols(2 * q + c)], cat.at[q, pl.ds(0, rows), :], load_sems.at[q]
        )

    def eye():
        i = lax.broadcasted_iota(jnp.int32, (rows, rows), 0)
        j = lax.broadcasted_iota(jnp.int32, (rows, rows), 1)
        return i == j

    def column(row):
        return jnp.sum(jnp.where(eye(), jnp.broadcast_to(row, (rows, rows)), 0.0), axis=1, keepdims=True)

    def row_of(col):
        return jnp.sum(jnp.where(eye(), jnp.broadcast_to(col, (rows, rows)), 0.0), axis=0, keepdims=True)

    slab = 2 * nx

    def start_rest():
        for q in range(nz * nx):
            dec_own(q).start()
            dec_send(q).start()
        pre_v[...] = jnp.zeros_like(pre_v)
        for load in loads:
            load.wait()

    def consume_acts(zz):
        acc = pre_v[...]
        for j in range(slab):
            i = zz * slab + j
            acc = acc + dot(enc_v[:, cols(i)], abuf[i], NT)
        pre_v[...] = acc

    def norms_and_counts():
        half = n // 2
        norms = []
        for m in range(2):
            def square(j, acc):
                w = dec_v[:, cols(m * half + j)].astype(f32)
                w = w * w
                for t in range(fb // 128):
                    acc = acc + w[:, t * 128:(t + 1) * 128]
                return acc
            acc = lax.fori_loop(0, half, square, jnp.zeros((rows, 128), f32))
            norms.append(jnp.sqrt(jnp.sum(acc, axis=1, keepdims=True) + norm_eps))
        active = lax.rem(mask_ref[...], 2).astype(f32)
        count = jnp.sum(active, axis=1, keepdims=True)
        lane = lax.broadcasted_iota(jnp.int32, (rows, 128), 1)
        coef_v[...] = jnp.where(
            lane == 0, sparsity_coef * count / norms[0],
            jnp.where(lane == 1, sparsity_coef * count / norms[1], norms[0] + norms[1]),
        )

    settle_acts = gather(abuf, a_up, a_x, a_sib, a_recv, consume_acts, lambda g: None, start_rest)

    active = lax.rem(mask_ref[...], 2).astype(f32)
    pre = pre_v[...] + column(encb_ref[...])
    feats = (active * pre).astype(bf16)
    feats2[pl.ds(0, rows), :] = feats
    fcopy = remote(
        feats2.at[pl.ds(0, rows), :], feats2.at[pl.ds(rows, rows), :], fsem.at[0], fsem.at[1], sib
    )
    fcopy.start()
    acts_copy = pltpu.make_async_copy(abuf, acts_out, out_sem.at[0])
    acts_copy.start()
    for q in range(nz * nx):
        dec_own(q).wait()
        dec_send(q).wait()
    fcopy.wait()

    both = feats2[...]

    def partial(q):
        return dot(both, cat[q], TN)

    piece = tokens // parts

    def lines(g):
        return pl.ds(pl.multiple_of(g * piece, piece), piece)

    def b_copy(k, zz, g, d):
        return remote(
            bsend.at[k * nx + d, lines(g), :], brecv.at[zz * nx + d, lines(g), :],
            b_s.at[k * nx + d, g], b_r.at[zz * nx + d, g], at(z, shifted_x(d), c),
        )

    def b_step(k, zz, g):
        for d in range(1, nx):
            @pl.when(g == 0)
            def _(d=d):
                bsend[k * nx + d] = partial(zz * nx + shifted_x(d)).astype(bf16)
            b_copy(k, zz, g, d).start()

    loop(events, lambda e: b_step(*farthest_first(e)))
    loop(parts, lambda g: b_step(0, z, g))
    for k in range(nz - 1, -1, -1):
        cpart[k] = partial(kth(k) * nx + x)
    settle_acts()
    norms_and_counts()

    def c_copies(k, zz, g):
        down_slot = zz + (nz - zz) * (zz == z - 1).astype(jnp.int32)
        return tuple(
            (go, remote(csend.at[k, lines(g), :], crecv.at[slot, lines(g), :], c_s.at[k, g], c_r.at[slot, g], device))
            for go, slot, device in ((zz > z, zz, at(z + 1, x, c)), (zz < z, down_slot, at(z - 1, x, c)))
        )

    def c_wait(slot, g):
        remote(csend.at[0, lines(g), :], crecv.at[slot, lines(g), :], c_s.at[0, g], c_r.at[slot, g], sib).wait_recv()

    def with_b(k, zz, g):
        part = cpart[k, lines(g), :]
        for d in range(1, nx):
            b_copy(k, zz, g, d).wait_recv()
            part = part + brecv[zz * nx + d, lines(g), :].astype(f32)
        return part

    def c_step(e):
        k, zz, g = farthest_first(e)
        part = with_b(k, zz, g)
        farther = jnp.logical_or(jnp.logical_and(zz > z, has_down), jnp.logical_and(zz < z, has_up))

        @pl.when(farther)
        def _():
            c_wait(zz, g)
            csend[k, lines(g), :] = (part + crecv[zz, lines(g), :].astype(f32)).astype(bf16)

        @pl.when(jnp.logical_not(farther))
        def _():
            csend[k, lines(g), :] = part.astype(bf16)

        for go, copy in c_copies(k, zz, g):
            @pl.when(go)
            def _(copy=copy):
                copy.start()

    loop(events, c_step)

    def prepare_error(piece):
        if piece == 0:
            return
        g = 2 - piece
        actst[lines(g), :] = with_b(0, z, g) + decb_ref[...] - actst[lines(g), :]

        @pl.when(has_down)
        def _():
            c_wait(z, g)
            actst[lines(g), :] += crecv[z, lines(g), :].astype(f32)

        @pl.when(has_up)
        def _():
            c_wait(nz, g)
            actst[lines(g), :] += crecv[nz, lines(g), :].astype(f32)

        ebuf[me, lines(g), :] = actst[lines(g), :].astype(bf16)

    def gd_copy(zz):
        w = cols(zz * slab, slab * fb)
        return pltpu.make_async_copy(gd_v.at[:, w], gd_out.at[:, w], gd_sem.at[zz])

    def finish_sums():
        gdb_out[...] = scale * jnp.sum(ebuf[me].astype(f32), axis=0, keepdims=True)
        grec_v[...] = jnp.zeros_like(grec_v)

        def settle(k, zz, g):
            for d in range(1, nx):
                b_copy(k, zz, g, d).wait_send()

        def settle_c(e):
            k, zz, g = farthest_first(e)
            settle(k, zz, g)
            for go, copy in c_copies(k, zz, g):
                @pl.when(go)
                def _(copy=copy):
                    copy.wait_send()

        loop(events, settle_c)
        loop(parts, lambda g: settle(0, z, g))

    def consume_errors(zz):
        own = feats2[pl.ds(0, rows), :]

        def body(j, acc):
            i = zz * slab + j
            e = ebuf[i]
            w = dec_v[:, cols(i)]
            acc = acc + dot(w, e, NT)
            adjusted = (i >= n // 2).astype(f32)
            coef = coef_v[:, 0:1] + adjusted * (coef_v[:, 1:2] - coef_v[:, 0:1])
            gd_v[:, cols(i)] = (scale * (dot(own, e, NN) + coef * w.astype(f32))).astype(bf16)
            return acc

        grec_v[...] = lax.fori_loop(0, slab, body, grec_v[...], unroll=True)
        gd_copy(zz).start()

    settle_errors = gather(ebuf, e_up, e_x, e_sib, e_recv, consume_errors, prepare_error, finish_sums)

    grec = grec_v[...]
    active = lax.rem(mask_ref[...], 2).astype(f32)
    gpre = (active * grec).astype(bf16)
    gpre_out[...] = gpre
    window = (mask_ref[...] // 2).astype(f32)
    theta = window * (column(thr_ref[...]) * grec + sparsity_coef * coef_v[:, 2:3])
    gth_out[...] = row_of(-(scale / spread) * jnp.sum(theta, axis=1, keepdims=True))
    geb_out[...] = row_of(scale * jnp.sum(gpre.astype(f32), axis=1, keepdims=True))
    settle_errors()
    acts_copy.wait()
    for zz in range(nz):
        gd_copy(zz).wait()


def finish(
    scale, acts_in, gpre_ref, gd_in, geb_ref, gth_ref, gdb_ref, ge_out, gd_out, geb_o, gth_o, gdb_o,
    acts_v, gd_v, ge_v, gd_r, gd_w, acts_r, ge_w,
):
    steps, strips = acts_r.shape[0], gd_r.shape[0]
    per, fb = acts_v.shape[0] // steps, acts_v.shape[2]
    tall = gd_v.shape[0] // strips

    def gd_read(i):
        rows = pl.ds(i * tall, tall)
        return pltpu.make_async_copy(gd_in.at[rows, :], gd_v.at[rows, :], gd_r.at[i])

    def gd_write(i):
        rows = pl.ds(i * tall, tall)
        return pltpu.make_async_copy(gd_v.at[rows, :], gd_out.at[rows, :], gd_w.at[i])

    def acts_read(i):
        some = pl.ds(i * per, per)
        return pltpu.make_async_copy(acts_in.at[some], acts_v.at[some], acts_r.at[i])

    def ge_write(i):
        w = pl.ds(i * per * fb, per * fb)
        return pltpu.make_async_copy(ge_v.at[:, w], ge_out.at[:, w], ge_w.at[i])

    for i in range(max(steps, strips)):
        if i < steps:
            acts_read(i).start()
        if i < strips:
            gd_read(i).start()
    geb_o[...] = geb_ref[...]
    gth_o[...] = gth_ref[...]
    gdb_o[...] = gdb_ref[...]
    for i in range(max(steps, strips)):
        if i < strips:
            gd_read(i).wait()
            gd_write(i).start()
        if i < steps:
            acts_read(i).wait()
            for j in range(i * per, (i + 1) * per):
                ge_v[:, j * fb:(j + 1) * fb] = (scale * dot(gpre_ref[...], acts_v[j], NN)).astype(bf16)
            ge_write(i).start()
    for i in range(strips):
        gd_write(i).wait()
    for i in range(steps):
        ge_write(i).wait()


def per_device(lat, acts, mask, enc_weight, enc_bias, threshold, dec_weight, dec_bias):
    nz, nx = lat_shape(lat)
    n = lat
    rows, tokens = mask.shape
    fb = acts.shape[0]
    width = dec_weight.shape[1]
    scale = 1.0 / math.sqrt(tokens)
    vmem = pl.BlockSpec(memory_space=pltpu.VMEM)
    hbm = pl.BlockSpec(memory_space=pl.ANY)
    parts = 2
    dma = pltpu.SemaphoreType.DMA
    outs = pl.pallas_call(
        functools.partial(kernel, nz, nx, parts, scale),
        out_shape=(
            jax.ShapeDtypeStruct((n, tokens, fb), bf16),
            jax.ShapeDtypeStruct((rows, tokens), bf16),
            jax.ShapeDtypeStruct((1, rows), f32),
            jax.ShapeDtypeStruct((1, rows), f32),
            jax.ShapeDtypeStruct((rows, width), bf16),
            jax.ShapeDtypeStruct((1, fb), f32),
        ),
        in_specs=[hbm] * 7,
        out_specs=(hbm, vmem, vmem, vmem, hbm, vmem),
        scratch_shapes=[
            pltpu.VMEM((fb, tokens), bf16),
            pltpu.VMEM((rows, tokens), jnp.int32),
            pltpu.VMEM((1, rows), f32),
            pltpu.VMEM((1, rows), f32),
            pltpu.VMEM((1, fb), f32),
            pltpu.VMEM((rows, width), bf16),
            pltpu.VMEM((rows, width), bf16),
            pltpu.VMEM((nz * nx, 2 * rows, fb), bf16),
            pltpu.VMEM((n, tokens, fb), bf16),
            pltpu.VMEM((n, tokens, fb), bf16),
            pltpu.VMEM((2 * rows, tokens), bf16),
            pltpu.VMEM((rows, tokens), f32),
            pltpu.VMEM((rows, tokens), f32),
            pltpu.VMEM((rows, 128), f32),
            pltpu.VMEM((nz * nx, tokens, fb), bf16),
            pltpu.VMEM((nz * nx, tokens, fb), bf16),
            pltpu.VMEM((nz, tokens, fb), bf16),
            pltpu.VMEM((nz + 1, tokens, fb), bf16),
            pltpu.VMEM((nz, tokens, fb), f32),
            pltpu.VMEM((rows, width), bf16),
            pltpu.VMEM((tokens, fb), f32),
            dma((7 + nz * nx,)), dma((nz * nx,)), dma((nz * nx,)), dma((2,)),
            dma((2, nx, nz * 3)), dma((nx, nz * 3)), dma((nx, nz * 3)), dma((n, 3)),
            dma((2, nx, nz * 3)), dma((nx, nz * 3)), dma((nx, nz * 3)), dma((n, 3)),
            dma((nz * nx, parts)), dma((nz * nx, parts)), dma((nz, parts)), dma((nz + 1, parts)),
            dma((nz,)), dma((1,)),
        ],
        compiler_params=pltpu.CompilerParams(
            collective_id=0, has_side_effects=True, vmem_limit_bytes=56 * 1024 * 1024
        ),
        name="crosscoder",
    )(
        acts, mask, enc_bias.reshape(1, rows), threshold.reshape(1, rows),
        dec_bias.reshape(1, fb), enc_weight, dec_weight,
    )
    all_acts, gpre, geb, gth, gd, gdb = outs
    steps, strips = 8, rows // 16
    ge, gd, geb, gth, gdb = pl.pallas_call(
        functools.partial(finish, scale),
        out_shape=(
            jax.ShapeDtypeStruct((rows, width), bf16),
            jax.ShapeDtypeStruct((rows, width), bf16),
            jax.ShapeDtypeStruct((1, rows), f32),
            jax.ShapeDtypeStruct((1, rows), f32),
            jax.ShapeDtypeStruct((1, fb), f32),
        ),
        in_specs=[hbm, vmem, hbm] + [vmem] * 3,
        out_specs=(hbm, hbm, vmem, vmem, vmem),
        scratch_shapes=[
            pltpu.VMEM((n, tokens, fb), bf16), pltpu.VMEM((rows, width), bf16), pltpu.VMEM((rows, width), bf16),
            dma((strips,)), dma((strips,)), dma((steps,)), dma((steps,)),
        ],
        compiler_params=pltpu.CompilerParams(vmem_limit_bytes=60 * 1024 * 1024),
        name="last_products",
    )(all_acts, gpre, gd, geb, gth, gdb)
    return ge, geb.reshape(rows), gth.reshape(rows), gd, gdb.reshape(fb)


def solution(mesh):
    wide, flat = P(("groups", "lat"), None), P(("groups", "lat"))
    return jax.shard_map(
        functools.partial(per_device, mesh.shape["lat"]), mesh=mesh,
        in_specs=(wide, wide, wide, flat, flat, wide, flat),
        out_specs=(wide, flat, flat, wide, flat), check_vma=False,
    )
```
